32 devices in a mesh: groups: 2 (over x), lat: 8 (over z, y), lon: 2 (over core).
Axes of the slice: x: 2, y: 2, z: 4, core: 2. Of those that a mesh axis runs over, the one named last changes fastest.
Arguments:
- state_field: bfloat16 [64, 1440, 256], P(('groups', 'lat'), 'lon'), parts along dimension 0, may hold values from -6 to 6
- heights: int32 [16], P(('groups', 'lat')), parts along dimension 0, may hold values from 1 to 4, 16 in all
- halo_widths: int32 [64], P(('groups', 'lat')), parts along dimension 0, may hold values from 1 to 8, as said below
- filter_values: bfloat16 [64, 3, 3, 17], P(('groups', 'lat')), parts along dimension 0, may hold values from -1.1953125 to 1.1953125
- weights_one: bfloat16 [3, 256, 256], replicated, may hold values from -0.21875 to 0.21875
- weights_two: bfloat16 [3, 256, 256], replicated, may hold values from -0.21875 to 0.21875
- cotangent: bfloat16 [64, 1440, 256], P(('groups', 'lat'), 'lon'), parts along dimension 0, may hold values from -6 to 6
Outputs:
- next_field: bfloat16 [64, 1440, 256], P(('groups', 'lat'), 'lon'), parts along dimension 0
- grad_field: bfloat16 [64, 1440, 256], P(('groups', 'lat'), 'lon'), parts along dimension 0
- grad_weights_one: float32 [6, 256, 256], P('groups'), parts along dimension 0
- grad_weights_two: float32 [6, 256, 256], P('groups'), parts along dimension 0
The draws below stay inside these ranges and needn't reach their ends.
There are 2 independent parts, one for each index of `groups`. The reference program is written for one: setup_inputs(seed, part) draws one part's arguments, and reference() takes and returns one part's arrays. A program takes and returns all parts, laid end to end along the dimension named above; an argument that names none is the same for every part. Nothing has to cross between parts.
Inputs may be any that keep to these rules, and one draw needn't show every extreme that they name: `heights`: the entries sum to 16 and one of them equals 4. `halo_widths`: slot 0 holds 8; values in slots that are not live are unused.
All inputs are finite; a program needn't handle non-finite values. No bound on the sum of `heights` on one device may be relied on, other than what follows from the above.
Results may differ from the reference program's by a relative error of at most 0.007.
Values may be sent and summed in bfloat16 or wider, within the bound.
No kernel may reach another device: no remote copies, remote signals or barrier semaphores. Data moves between devices by JAX's collectives and lax.ppermute only.
A program may use at most 64 MiB of HBM per device.

```python
import math
import jax
import jax.numpy as jnp
import numpy as np
from jax import lax

C = 256
NLON = 1440
K = 3
HALO = 8
CAP = 4
NLAT = 16
SLOTS = 32
N_LAT = 8


def draw_halo_widths(key, part):
    key = jax.random.fold_in(key, 7)
    widths = jax.random.randint(key, (SLOTS,), 1, HALO + 1, dtype=jnp.int32)
    return widths.at[0].set(HALO)


def levels(key, extent, pieces, low, high):
    level = 1.0
    for axis_at, shards_of in pieces:
        draws = jax.random.uniform(jax.random.fold_in(jax.random.fold_in(key, 6), axis_at), (shards_of,), jnp.float32, low / len(pieces), high / len(pieces))
        level = level * jnp.repeat(jnp.exp(draws), extent[axis_at] // shards_of).reshape((-1,) + (1,) * (len(extent) - 1 - axis_at))
    return level


def length_profile(number_of, total, limit, skew):
    portions = [(1 << 20) // math.isqrt(rank ** skew) + 1 for rank in range(2, number_of + 1)]
    spare, counts = total - limit - (number_of - 1), [1] * (number_of - 1)
    while spare > 0:
        movable = [i for i in range(number_of - 1) if counts[i] < limit]
        mass, left = sum([portions[i] for i in movable]), spare
        for i in movable:
            addition = min(limit - counts[i], max(1, left * portions[i] // mass), spare)
            counts[i] = counts[i] + addition
            spare = spare - addition
    return np.array([limit] + counts)


def ragged_sizes(rng, count, total, limit, lean):
    if count == 2:
        one = jax.random.randint(rng, (), max(1, total - limit), min(limit, total - 1) + 1)
        return jnp.stack([one, total - one])
    tallies = jnp.asarray(length_profile(count, total, limit, lean), jnp.int32)
    couples = (count - 1) // 2
    source_of, taker = tallies[1:1 + 2 * couples:2], tallies[2:2 + 2 * couples:2]
    slack = jnp.minimum(source_of - 1, limit - taker)
    passed = jax.random.randint(jax.random.fold_in(rng, 1), (couples,), 0, 1 << 20) % (slack + 1)
    tallies = tallies.at[1:1 + 2 * couples:2].set(source_of - passed).at[2:2 + 2 * couples:2].set(taker + passed)
    return tallies[jax.random.permutation(jax.random.fold_in(rng, 2), count)]


def centred(stream_key, shape, spread, limit, shards=(), held_as=jnp.bfloat16):
    array = spread * jax.random.normal(stream_key, shape, jnp.float32)
    if shards:
        array = array * levels(stream_key, shape, shards, -0.22, 0.18)
    return jnp.clip(array, -limit, limit).astype(held_as)


def setup_inputs(seed: int = 0, part: int = 0) -> dict:
    splits = jax.random.split(jax.random.key(seed), 8)
    part_splits = jax.random.split(jax.random.fold_in(splits[7], part), 8)
    return {
        "state_field": centred(part_splits[0], (SLOTS, NLON, C), 1.0, 6.0, ((0, 8), (1, 2))),
        "heights": ragged_sizes(part_splits[1], N_LAT, NLAT, CAP, 2).astype(jnp.int32),
        "halo_widths": draw_halo_widths(jax.random.fold_in(jax.random.fold_in(splits[7], part), 71), part),
        "filter_values": centred(part_splits[3], (SLOTS, K, 3, 2 * HALO + 1), 0.2, 1.1953125, ((0, 8),)),
        "weights_one": centred(splits[4], (K, C, C), (K * C) ** -0.5, 0.21875),
        "weights_two": centred(splits[5], (K, C, C), (K * C) ** -0.5, 0.21875),
        "cotangent": centred(part_splits[6], (SLOTS, NLON, C), 1.0, 6.0, ((0, 8), (1, 2))),
    }


def gelu_slope(values):
    inner = 0.5 * (1.0 + jax.scipy.special.erf(values * (1.0 / math.sqrt(2.0))))
    return inner + values * jnp.exp(-0.5 * values * values) * (1.0 / math.sqrt(2.0 * math.pi))

def slot_layout(heights):
    starts = (jnp.cumsum(heights) - heights).astype(jnp.int32)
    slot_ids = jnp.arange(CAP, dtype=jnp.int32)
    live_mask = slot_ids[None, :] < heights[:, None]
    grid_row = starts[:, None] + slot_ids[None, :]
    target = jnp.where(live_mask, grid_row, NLAT).reshape(-1).astype(jnp.int32)
    source = jnp.where(live_mask, grid_row, 0).reshape(-1).astype(jnp.int32)
    return (live_mask.reshape(-1), target, source)

def stencil(grid_field, filter_coef):
    padded = jnp.pad(grid_field, ((1, 1), (0, 0), (0, 0)))
    padded = jnp.concatenate([padded[:, NLON - HALO:], padded, padded[:, :HALO]], axis=1)

    def one_row(row_index):
        nearby = lax.dynamic_slice_in_dim(padded, row_index, 3, 0)
        windows = jnp.stack([nearby[:, lon_step:lon_step + NLON] for lon_step in range(2 * HALO + 1)], axis=1)
        return jnp.einsum('kab,abjc->kjc', filter_coef[row_index], windows, precision=lax.Precision.HIGHEST)
    mapped = lax.map(one_row, jnp.arange(NLAT, dtype=jnp.int32))
    return jnp.moveaxis(mapped, 0, 1)

def reference(state_field, heights, halo_widths, filter_values, weights_one, weights_two, cotangent):
    live_mask, target, source = slot_layout(heights)

    def to_grid(values):
        return jnp.zeros((NLAT,) + values.shape[1:], values.dtype).at[target].set(values, mode='drop')

    def to_slots(values):
        taken = values[source]
        shaped = live_mask.reshape((-1,) + (1,) * (values.ndim - 1))
        return jnp.where(shaped, taken, jnp.zeros_like(taken))
    offsets = jnp.abs(jnp.arange(2 * HALO + 1, dtype=jnp.int32) - HALO)
    inside = offsets[None, :] <= halo_widths[:, None]
    masked = jnp.where(inside[:, None, None, :], filter_values, jnp.zeros_like(filter_values))
    filter_coef = to_grid(masked).astype(jnp.float32)

    def filter_grid(values):
        return stencil(values, filter_coef)
    grid_field = to_grid(state_field).astype(jnp.float32)
    basis_one = filter_grid(grid_field).astype(jnp.bfloat16)
    pre_one = jnp.einsum('kijc,kcd->ijd', basis_one.astype(jnp.float32), weights_one.astype(jnp.float32))
    hidden = jax.nn.gelu(pre_one, approximate=False).astype(jnp.bfloat16)
    basis_two = filter_grid(hidden.astype(jnp.float32)).astype(jnp.bfloat16)
    next_field = jnp.einsum('kijc,kcd->ijd', basis_two.astype(jnp.float32), weights_two.astype(jnp.float32)).astype(jnp.bfloat16)
    grad_scale = 1.0 / math.sqrt(NLAT * NLON)
    grid_cot = to_grid(cotangent).astype(jnp.float32)
    grad_weights_two = grad_scale * jnp.einsum('kijc,ijd->kcd', basis_two.astype(jnp.float32), grid_cot)
    back_two = jnp.einsum('ijd,kcd->kijc', grid_cot, weights_two.astype(jnp.float32)).astype(jnp.bfloat16)
    unused, adjoint = jax.vjp(filter_grid, grid_field)
    grad_hidden = adjoint(back_two.astype(jnp.float32))[0]
    grad_pre = (grad_hidden * gelu_slope(pre_one)).astype(jnp.bfloat16)
    grad_weights_one = grad_scale * jnp.einsum('kijc,ijd->kcd', basis_one.astype(jnp.float32), grad_pre.astype(jnp.float32))
    back_one = jnp.einsum('ijd,kcd->kijc', grad_pre.astype(jnp.float32), weights_one.astype(jnp.float32)).astype(jnp.bfloat16)
    grad_field = adjoint(back_one.astype(jnp.float32))[0].astype(jnp.bfloat16)
    return (to_slots(next_field), to_slots(grad_field), grad_weights_one, grad_weights_two)
```

```python
import functools
import math

import jax
import jax.numpy as jnp
from jax import lax
from jax.experimental import pallas as pl
from jax.experimental.pallas import tpu as pltpu
from jax.sharding import PartitionSpec as P

NLON = 1440
HALO = 8
ROWS = 2
EDGE = 2 * HALO
TILE = 48
WINDOW = TILE + 2 * EDGE
LANES = 256
CHUNK_TILES = 5
VMEM_LIMIT = 40 * 1024 * 1024


def copy_halos(odd, height, ev_ref, od_ref, xe_ref, lon_count):
    def place(src_ref, slot):
        edge = src_ref[lon_count : lon_count + EDGE, :]
        xe_ref[slot, 0:EDGE, :] = edge
        xe_ref[slot, EDGE : EDGE + lon_count, :] = src_ref[0:lon_count, :]
        xe_ref[slot, EDGE + lon_count : 2 * EDGE + lon_count, :] = edge

    @pl.when(odd == 1)
    def _():
        place(ev_ref, 0)
        place(od_ref, height + 1)

    @pl.when(odd == 0)
    def _():
        place(od_ref, 0)
        place(ev_ref, height + 1)


def stage_kernel(mode, info_ref, x_ref, edge_ref, ev_ref, od_ref, mix_ref, *refs):
    channels = x_ref.shape[2]
    slots, lon_count = x_ref.shape[:2]
    height, odd = info_ref[0], info_ref[1]
    if mode == "first":
        coef_ref, basis_ref, hidden_ref, slope_ref, band_ref, xe_ref = refs
    elif mode == "back":
        coef_ref, slope_ref, basis_ref, out_ref, band_ref, xe_ref, ext_ref = refs
    else:
        band_ref, out_ref, basis_ref, xe_ref = refs

    xe_ref[1 : slots + 1, 0:EDGE, :] = edge_ref[...]
    xe_ref[1 : slots + 1, EDGE : EDGE + lon_count, :] = x_ref[...]
    xe_ref[1 : slots + 1, EDGE + lon_count : 2 * EDGE + lon_count, :] = edge_ref[...]
    copy_halos(odd, height, ev_ref, od_ref, xe_ref, lon_count)

    if mode == "back":
        start = lon_count + EDGE
        ext_ref[1 : slots + 1] = coef_ref[...]

        def place(src_ref, slot):
            ext_ref[slot] = src_ref[start : start + EDGE, :].astype(jnp.float32)[0:8]

        @pl.when(odd == 1)
        def _():
            place(ev_ref, 0)
            place(od_ref, height + 1)

        @pl.when(odd == 0)
        def _():
            place(od_ref, 0)
            place(ev_ref, height + 1)

    zeros_tail = jnp.zeros((LANES - 3 * WINDOW, channels), jnp.bfloat16)
    chunk = CHUNK_TILES * TILE

    def one_row(row, carry):
        if mode == "first":
            base = coef_ref[row]
        elif mode == "back":
            lane = lax.broadcasted_iota(jnp.int32, (8, LANES), 1)
            base = jnp.where(
                lane < WINDOW,
                ext_ref[row],
                jnp.where(lane < 2 * WINDOW, ext_ref[row + 1], ext_ref[row + 2]),
            )
        if mode != "last":
            for k in range(3):
                spread = jnp.broadcast_to(base[k : k + 1], (TILE, LANES))
                rolled = pltpu.roll(spread, 0, 1, stride=1, stride_axis=0)
                band_ref[row, k * TILE : (k + 1) * TILE, :] = rolled.astype(jnp.bfloat16)

        def one_chunk(chunk_index, inner):
            begin = pl.multiple_of(chunk_index * chunk, chunk)
            band = band_ref[row]
            for tile in range(CHUNK_TILES):
                at = begin + tile * TILE
                window = jnp.concatenate(
                    [xe_ref[row + lat_step, pl.ds(at, WINDOW), :] for lat_step in range(3)]
                    + [zeros_tail],
                    axis=0,
                )
                summed = jnp.dot(band, window, preferred_element_type=jnp.float32)
                summed = summed.astype(jnp.bfloat16)
                for k in range(3):
                    piece = summed[k * TILE : (k + 1) * TILE]
                    if mode == "last":
                        basis_ref[pl.ds(at, TILE), k * channels : (k + 1) * channels] = piece
                    else:
                        basis_ref[row, pl.ds(at, TILE), k * channels : (k + 1) * channels] = piece
            if mode == "last":
                terms = basis_ref[pl.ds(begin, chunk), :]
            else:
                terms = basis_ref[row, pl.ds(begin, chunk), :]
            mixed = jnp.dot(terms, mix_ref[...], preferred_element_type=jnp.float32)
            if mode == "first":
                cdf = 0.5 * (1.0 + lax.erf(mixed * (1.0 / math.sqrt(2.0))))
                pdf = jnp.exp(-0.5 * mixed * mixed) * (1.0 / math.sqrt(2.0 * math.pi))
                hidden_ref[row, pl.ds(begin, chunk), :] = (mixed * cdf).astype(jnp.bfloat16)
                slope_ref[row, pl.ds(begin, chunk), :] = cdf + mixed * pdf
            elif mode == "back":
                slope = slope_ref[row, pl.ds(begin, chunk), :]
                out_ref[row, pl.ds(begin, chunk), :] = (mixed * slope).astype(jnp.bfloat16)
            else:
                out_ref[row, pl.ds(begin, chunk), :] = mixed.astype(jnp.bfloat16)
            return inner

        return lax.fori_loop(0, lon_count // chunk, one_chunk, carry)

    lax.fori_loop(0, height, one_row, 0)
    if mode == "last":

        def clear(row, carry):
            out_ref[row] = jnp.zeros(out_ref.shape[1:], out_ref.dtype)
            return carry

        lax.fori_loop(height, slots, clear, 0)


def stage(mode, info, x, edge, ev, od, mix, *extra):
    slots, lon_count, channels = x.shape
    bf16, f32 = jnp.bfloat16, jnp.float32
    basis = jax.ShapeDtypeStruct((slots, lon_count, 3 * channels), bf16)
    field = jax.ShapeDtypeStruct(x.shape, bf16)
    slope = jax.ShapeDtypeStruct(x.shape, f32)
    band = jax.ShapeDtypeStruct((slots, 3 * TILE, LANES), bf16)
    scratch = [pltpu.VMEM((slots + 2, lon_count + 2 * EDGE, channels), bf16)]
    if mode == "first":
        outs = (basis, field, slope, band)
    elif mode == "back":
        outs = (basis, field, band)
        scratch.append(pltpu.VMEM((slots + 2, 8, LANES), f32))
    else:
        outs = (field,)
        scratch.insert(0, pltpu.VMEM((lon_count, 3 * channels), bf16))
    points = slots * lon_count
    flops = 2 * points * channels * (9 * WINDOW + 3 * channels)
    return pl.pallas_call(
        functools.partial(stage_kernel, mode),
        out_shape=outs,
        in_specs=[pl.BlockSpec(memory_space=pltpu.SMEM)]
        + [pl.BlockSpec(memory_space=pltpu.VMEM)] * (5 + len(extra)),
        out_specs=tuple(pl.BlockSpec(memory_space=pltpu.VMEM) for _ in outs),
        scratch_shapes=scratch,
        compiler_params=pltpu.CompilerParams(vmem_limit_bytes=VMEM_LIMIT),
        cost_estimate=pl.CostEstimate(
            flops=flops, bytes_accessed=points * channels * 8, transcendentals=0
        ),
    )(info, x, edge, ev, od, mix, *extra)


def grads_kernel(scale, info_ref, basis_ref, grad_ref, hidden_ref, terms_ref, one_ref, two_ref, acc_one, acc_two):
    channels = grad_ref.shape[2]
    height = info_ref[0]
    acc_one[...] = jnp.zeros_like(acc_one)
    acc_two[...] = jnp.zeros_like(acc_two)

    def one_row(row, carry):
        grad_t = grad_ref[row].T
        hidden_t = hidden_ref[row].T
        for k in range(3):
            span = slice(k * channels, (k + 1) * channels)
            acc_one[:, span] += jnp.dot(grad_t, basis_ref[row, :, span], preferred_element_type=jnp.float32)
            acc_two[:, span] += jnp.dot(hidden_t, terms_ref[row, :, span], preferred_element_type=jnp.float32)
        return carry

    lax.fori_loop(0, height, one_row, 0)
    for k in range(3):
        span = slice(k * channels, (k + 1) * channels)
        one_ref[k] = acc_one[:, span].T * scale
        two_ref[k] = acc_two[:, span] * scale


def weight_grads(scale, info, basis, grad, hidden, terms):
    channels = grad.shape[2]
    out = jax.ShapeDtypeStruct((3, channels, channels), jnp.float32)
    acc = pltpu.VMEM((channels, 3 * channels), jnp.float32)
    points = grad.shape[0] * grad.shape[1]
    return pl.pallas_call(
        functools.partial(grads_kernel, scale),
        out_shape=(out, out),
        in_specs=[pl.BlockSpec(memory_space=pltpu.SMEM)] + [pl.BlockSpec(memory_space=pltpu.VMEM)] * 4,
        out_specs=(pl.BlockSpec(memory_space=pltpu.VMEM),) * 2,
        scratch_shapes=[acc, acc],
        compiler_params=pltpu.CompilerParams(vmem_limit_bytes=VMEM_LIMIT),
        cost_estimate=pl.CostEstimate(
            flops=12 * points * channels * channels, bytes_accessed=points * channels * 16, transcendentals=0
        ),
    )(info, basis, grad, hidden, terms)


def coef_lanes(coef):
    slots, basis_count, steps, spans = coef.shape
    wide = jnp.pad(coef, ((0, 0), (0, 0), (0, 0), (HALO, WINDOW - HALO - spans)))
    wide = wide.reshape(slots, basis_count, steps * WINDOW)
    return jnp.pad(wide, ((0, 0), (0, 8 - basis_count), (0, LANES - steps * WINDOW)))


def lon_edges(x):
    lon_count = x.shape[1]
    edges = jnp.concatenate([x[:, :HALO], x[:, lon_count - HALO :]], axis=1)
    return lax.ppermute(edges, "lon", [(0, 1), (1, 0)])


def row_swap(x, edges, height, extra=None):
    size = lax.axis_size("lat")
    even = lax.rem(lax.axis_index("lat"), 2) == 0
    last = height - 1
    routes = ([(i, i ^ 1) for i in range(size)], [(i, (i + 1 if i % 2 else i - 1)) for i in range(1, size - 1)])
    swapped = []
    for route, row in zip(routes, (jnp.where(even, last, 0), jnp.where(even, 0, last)), strict=True):
        parts = [
            lax.dynamic_index_in_dim(x, row, 0, keepdims=False),
            lax.dynamic_index_in_dim(edges, row, 0, keepdims=False),
        ]
        if extra is not None:
            parts.append(lax.dynamic_index_in_dim(extra, row, 0, keepdims=False))
        swapped.append(lax.ppermute(jnp.concatenate(parts, axis=0), "lat", route))
    return swapped


def total(one, two):
    size = lax.axis_size("lat")
    low = size // 4
    core = lax.axis_index("lon")
    place = lax.axis_index("lat") // low
    shape = one.shape
    rows = shape[0] * shape[1] // 4
    bf16, f32 = jnp.bfloat16, jnp.float32
    other = jnp.where(core == 0, two, one).astype(bf16)
    mine = jnp.where(core == 0, one, two)
    mine = mine + lax.ppermute(other, "lon", [(0, 1), (1, 0)]).astype(f32)
    mine = mine.reshape(4, rows, shape[2])

    def across(value, step):
        return lax.ppermute(value, "lat", [(i, ((i // low) ^ step) * low + i % low) for i in range(size)])

    sums = lax.dynamic_index_in_dim(mine, place, 0, keepdims=False)
    for step in (1, 2, 3):
        piece = lax.dynamic_index_in_dim(mine, place ^ step, 0, keepdims=False).astype(bf16)
        sums = sums + across(piece, step).astype(f32)
    stride = 1
    while stride < low:
        held = sums.astype(bf16)
        sums = held.astype(f32) + lax.ppermute(held, "lat", [(i, i ^ stride) for i in range(size)]).astype(f32)
        stride *= 2
    done = sums.astype(bf16)
    whole = jnp.zeros((4, rows, shape[2]), bf16)
    whole = lax.dynamic_update_index_in_dim(whole, done, place, 0)
    for step in (1, 2, 3):
        whole = lax.dynamic_update_index_in_dim(whole, across(done, step), place ^ step, 0)
    theirs = lax.ppermute(whole, "lon", [(0, 1), (1, 0)])
    first = jnp.where(core == 0, whole, theirs).reshape(shape).astype(f32)
    second = jnp.where(core == 0, theirs, whole).reshape(shape).astype(f32)
    return first, second


def per_device(state_field, heights, halo_widths, filter_values, weights_one, weights_two, cotangent):
    height = heights[0]
    spans = filter_values.shape[-1]
    channels = state_field.shape[2]
    bf16 = jnp.bfloat16
    odd = lax.rem(lax.axis_index("lat"), 2)
    info = jnp.stack([height, odd]).astype(jnp.int32)

    offsets = jnp.abs(jnp.arange(spans, dtype=jnp.int32) - (spans - 1) // 2)
    inside = offsets[None, :] <= halo_widths[:, None]
    coef = jnp.where(inside[:, None, None, :], filter_values, jnp.zeros_like(filter_values))
    forward = coef_lanes(coef).astype(jnp.float32)
    backward = coef_lanes(coef[:, :, ::-1, ::-1])
    backward_tile = jnp.pad(backward, ((0, 0), (0, EDGE - 8), (0, 0)))

    edges_s = lon_edges(state_field)
    edges_c = lon_edges(cotangent)
    state_ev, state_od = row_swap(state_field, edges_s, height)
    cot_ev, cot_od = row_swap(cotangent, edges_c, height, backward_tile)

    mix_one = weights_one.reshape(3 * channels, channels)
    mix_two = weights_two.reshape(3 * channels, channels)
    mix_one_t = jnp.swapaxes(weights_one, 1, 2).reshape(3 * channels, channels)
    mix_two_t = jnp.swapaxes(weights_two, 1, 2).reshape(3 * channels, channels)

    basis_one, hidden, slope, band = stage("first", info, state_field, edges_s, state_ev, state_od, mix_one, forward)
    edges_h = lon_edges(hidden)
    hidden_ev, hidden_od = row_swap(hidden, edges_h, height)

    terms, grad_pre, band_t = stage(
        "back", info, cotangent, edges_c, cot_ev, cot_od, mix_two_t, backward.astype(jnp.float32), slope
    )
    edges_g = lon_edges(grad_pre)
    grad_ev, grad_od = row_swap(grad_pre, edges_g, height)

    scale = 1.0 / math.sqrt(ROWS * lax.axis_size("lat") * NLON)
    local_one, local_two = weight_grads(scale, info, basis_one, grad_pre, hidden, terms)
    grad_one, grad_two = total(local_one, local_two)

    (next_field,) = stage("last", info, hidden, edges_h, hidden_ev, hidden_od, mix_two, band)
    (grad_field,) = stage("last", info, grad_pre, edges_g, grad_ev, grad_od, mix_one_t, band_t)
    return next_field, grad_field, grad_one, grad_two


def solution(mesh):
    in_specs = (
        P(("groups", "lat"), "lon", None),
        P(("groups", "lat")),
        P(("groups", "lat")),
        P(("groups", "lat"), None, None, None),
        P(),
        P(),
        P(("groups", "lat"), "lon", None),
    )
    out_specs = (
        P(("groups", "lat"), "lon", None),
        P(("groups", "lat"), "lon", None),
        P("groups", None, None),
        P("groups", None, None),
    )
    return jax.shard_map(
        per_device, mesh=mesh, in_specs=in_specs, out_specs=out_specs, check_vma=False
    )
```

```python
import functools
import math

import jax
import jax.numpy as jnp
from jax import lax
from jax.experimental import pallas as pl
from jax.experimental.pallas import tpu as pltpu
from jax.sharding import PartitionSpec as P

NLON = 1440
HALO = 8
ROWS = 2
EDGE = 2 * HALO
TILE = 48
WINDOW = TILE + 2 * EDGE
LANES = 256
CHUNKS = 3
VMEM_LIMIT = 14 * 1024 * 1024
SMALL_LIMIT = 6 * 1024 * 1024


def cost(flops, bytes_accessed):
    return pl.CostEstimate(flops=flops, bytes_accessed=bytes_accessed, transcendentals=0)


def stage_kernel(mode, scale, *refs):
    info_ref, x_ref, ev_ref, od_ref, mix_ref = refs[:5]
    slots, channels = x_ref.shape[0], x_ref.shape[2]
    wide = ev_ref.shape[0] + {"first": 2 * EDGE, "back": -EDGE, "last": 0}[mode]
    lon_count = wide - 2 * EDGE
    height, odd = info_ref[0], info_ref[1]
    own = slice(EDGE, EDGE + lon_count)
    if mode == "first":
        edge_ref, halo_ref, coef_ref, basis_ref, out_ref, slope_ref, ev_out, od_out, band_ref, xe_ref = refs[5:]
    elif mode == "back":
        edge_ref, coef_ref, slope_ref, basis_ref, hidden_ref = refs[5:10]
        out_ref, ext_ref, ev_out, od_out, mine_ref, other_ref = refs[10:16]
        band_ref, terms_ref, xe_ref, acc_one, acc_two = refs[16:]
    else:
        coef_ref, out_ref, band_ref, terms_ref, xe_ref = refs[5:]

    def each_live(act):
        def step(row, carry):
            act(row)
            return carry

        lax.fori_loop(0, height, step, 0)

    def load(row):
        if mode == "last":
            xe_ref[row + 1] = x_ref[row]
        else:
            xe_ref[row + 1, 0:EDGE, :] = edge_ref[row, EDGE : 2 * EDGE, :]
            xe_ref[row + 1, own, :] = x_ref[row]
            xe_ref[row + 1, EDGE + lon_count : wide, :] = edge_ref[row, 0:EDGE, :]

    def load_halo(src_ref, at, slot):
        if mode == "first":
            xe_ref[slot, 0:EDGE, :] = halo_ref[at + EDGE : at + 2 * EDGE, :]
            xe_ref[slot, own, :] = src_ref[...]
            xe_ref[slot, EDGE + lon_count : wide, :] = halo_ref[at : at + EDGE, :]
        else:
            xe_ref[slot] = src_ref[0:wide, :]
        if mode == "back":
            ext_ref[slot] = src_ref[wide : wide + EDGE, :].astype(jnp.float32)[0:8]

    each_live(load)
    if mode == "back":
        ext_ref[1 : slots + 1] = coef_ref[...]
        acc_one[...] = jnp.zeros_like(acc_one)
        acc_two[...] = jnp.zeros_like(acc_two)

    @pl.when(odd == 1)
    def _():
        load_halo(ev_ref, 0, 0)
        load_halo(od_ref, 2 * EDGE, height + 1)

    @pl.when(odd == 0)
    def _():
        load_halo(od_ref, 2 * EDGE, 0)
        load_halo(ev_ref, 0, height + 1)

    zeros_tail = jnp.zeros((LANES - 3 * WINDOW, channels), jnp.bfloat16)
    tiles = lon_count // TILE
    chunk = -(-tiles // CHUNKS)

    def one_row(row):
        rows_ref = ext_ref if mode == "back" else coef_ref
        if rows_ref.shape[0] == slots:
            base = rows_ref[row]
        else:
            lane = lax.broadcasted_iota(jnp.int32, (8, LANES), 1)
            base = jnp.where(
                lane < WINDOW,
                rows_ref[row],
                jnp.where(lane < 2 * WINDOW, rows_ref[row + 1], rows_ref[row + 2]),
            )
        for k in range(3):
            spread = jnp.broadcast_to(base[k : k + 1], (WINDOW, LANES))
            rolled = pltpu.roll(spread, LANES - EDGE, 1, stride=1, stride_axis=0)
            band_ref[row, k * WINDOW : (k + 1) * WINDOW, :] = rolled.astype(jnp.bfloat16)

        def emit(first_tile, last_tile):
            begin, end = EDGE + first_tile * TILE, EDGE + last_tile * TILE
            if mode != "last":
                begin -= EDGE * (first_tile == 0)
                end += EDGE * (last_tile == tiles)
            for tile in range(first_tile, last_tile):
                window = jnp.concatenate(
                    [xe_ref[row + lat_step, tile * TILE : tile * TILE + WINDOW, :] for lat_step in range(3)]
                    + [zeros_tail],
                    axis=0,
                )
                low, high = EDGE, EDGE + TILE
                if mode != "last":
                    low -= EDGE * (tile == 0)
                    high += EDGE * (tile == tiles - 1)
                size = high - low
                band = jnp.concatenate(
                    [band_ref[row, k * WINDOW + low : k * WINDOW + high, :] for k in range(3)], axis=0
                )
                summed = jnp.dot(band, window, preferred_element_type=jnp.float32).astype(jnp.bfloat16)
                for k in range(3):
                    piece = summed[k * size : (k + 1) * size]
                    at = tile * TILE + low
                    span = slice(k * channels, (k + 1) * channels)
                    if mode == "first":
                        basis_ref[row, at : at + size, span] = piece
                    else:
                        terms_ref[at : at + size, span] = piece
            terms = basis_ref[row, begin:end, :] if mode == "first" else terms_ref[begin:end, :]
            mixed = jnp.dot(terms, mix_ref[...], preferred_element_type=jnp.float32)
            if mode == "first":
                cdf = 0.5 * (1.0 + lax.erf(mixed * (1.0 / math.sqrt(2.0))))
                pdf = jnp.exp(-0.5 * mixed * mixed) * (1.0 / math.sqrt(2.0 * math.pi))
                out_ref[row, begin:end, :] = (mixed * cdf).astype(jnp.bfloat16)
                slope_ref[row, begin:end, :] = cdf + mixed * pdf
            elif mode == "back":
                out_ref[row, begin:end, :] = (mixed * slope_ref[row, begin:end, :]).astype(jnp.bfloat16)
            else:
                out_ref[row, begin - EDGE : end - EDGE, :] = mixed.astype(jnp.bfloat16)

        for first_tile in range(0, tiles, chunk):
            emit(first_tile, min(first_tile + chunk, tiles))
        if mode == "back":
            grad_t = out_ref[row, own, :].T
            hidden_t = hidden_ref[row, own, :].T
            for k in range(3):
                span = slice(k * channels, (k + 1) * channels)
                acc_one[:, span] += jnp.dot(grad_t, basis_ref[row, own, span], preferred_element_type=jnp.float32)
                acc_two[:, span] += jnp.dot(hidden_t, terms_ref[own, span], preferred_element_type=jnp.float32)

    each_live(one_row)
    if mode == "last":

        def clear(row, carry):
            out_ref[row] = jnp.zeros(out_ref.shape[1:], out_ref.dtype)
            return carry

        lax.fori_loop(height, slots, clear, 0)
    else:
        ev_out[...] = out_ref[info_ref[2]]
        od_out[...] = out_ref[info_ref[3]]
        if mode == "back":

            def write(one_ref, two_ref):
                for k in range(3):
                    span = slice(k * channels, (k + 1) * channels)
                    one_ref[span] = (acc_one[:, span].T * scale).astype(one_ref.dtype)
                    two_ref[span] = (acc_two[:, span] * scale).astype(two_ref.dtype)

            @pl.when(info_ref[4] == 0)
            def _():
                write(mine_ref, other_ref)

            @pl.when(info_ref[4] != 0)
            def _():
                write(other_ref, mine_ref)


def stage(mode, estimate, info, x, ev, od, mix, *extra, scale=None):
    slots, channels = x.shape[0], x.shape[2]
    wide = ev.shape[0] + {"first": 2 * EDGE, "back": -EDGE, "last": 0}[mode]
    lon_count = wide - 2 * EDGE
    bf16, f32 = jnp.bfloat16, jnp.float32
    vmem = pl.BlockSpec(memory_space=pltpu.VMEM)
    basis = ((slots, wide, 3 * channels), bf16)
    field = ((slots, wide, channels), bf16)
    slope = ((slots, wide, channels), f32)
    band = ((slots, 3 * WINDOW, LANES), bf16)
    row = ((wide, channels), bf16)
    terms = ((wide, 3 * channels), bf16)
    ext = ((slots + 2, wide, channels), bf16)
    sums = (3 * channels, channels)
    if mode == "first":
        outs = (basis, field, slope, row, row)
        scratch = [band, ext]
    elif mode == "back":
        outs = (field, ((slots + 2, 8, LANES), f32), row, row, (sums, f32), (sums, bf16))
        acc = ((channels, 3 * channels), f32)
        scratch = [band, terms, ext, acc, acc]
    else:
        outs = (((slots, lon_count, channels), bf16),)
        scratch = [band, terms, ext]
    return pl.pallas_call(
        functools.partial(stage_kernel, mode, scale),
        out_shape=tuple(jax.ShapeDtypeStruct(*array) for array in outs),
        in_specs=[pl.BlockSpec(memory_space=pltpu.SMEM)] + [vmem] * (4 + len(extra)),
        out_specs=(vmem,) * len(outs),
        scratch_shapes=[pltpu.VMEM(*array) for array in scratch],
        compiler_params=pltpu.CompilerParams(vmem_limit_bytes=VMEM_LIMIT),
        cost_estimate=estimate,
    )(info, x, ev, od, mix, *extra)


def pack_kernel(which, info_ref, x_ref, edge_ref, tile_ref, out_ref, sem):
    lon_count = x_ref.shape[1]
    wide = lon_count + 2 * EDGE
    row = info_ref[which]
    copy = pltpu.make_async_copy(x_ref.at[row], out_ref.at[EDGE : EDGE + lon_count], sem)
    copy.start()
    out_ref[0:EDGE] = edge_ref[row, EDGE : 2 * EDGE]
    out_ref[EDGE + lon_count : wide] = edge_ref[row, 0:EDGE]
    out_ref[wide : wide + EDGE] = tile_ref[row]
    copy.wait()


def pack(which, info, x, edges, tiles, after=()):
    row = jax.ShapeDtypeStruct((x.shape[1] + 3 * EDGE, x.shape[2]), x.dtype)
    kernel = functools.partial(pack_kernel, which)
    (out,) = local_call(
        kernel, info, (row,), SMALL_LIMIT, cost(0, 4 * row.size), (edges, tiles), (pltpu.SemaphoreType.DMA,), (x,), after
    )
    return out


def local_call(kernel, info, outs, limit, estimate, operands, scratch=(), far=(), after=()):
    vmem, anywhere = pl.BlockSpec(memory_space=pltpu.VMEM), pl.BlockSpec(memory_space=pl.ANY)

    def body(info_ref, *refs):
        kernel(info_ref, *refs[len(after) :])

    return pl.pallas_call(
        body,
        out_shape=tuple(outs),
        in_specs=[pl.BlockSpec(memory_space=pltpu.SMEM)]
        + [anywhere] * (len(after) + len(far))
        + [vmem] * len(operands),
        out_specs=(vmem,) * len(outs),
        scratch_shapes=list(scratch),
        compiler_params=pltpu.CompilerParams(vmem_limit_bytes=limit),
        cost_estimate=estimate,
    )(info, *after, *far, *operands)


def pass_kernel(info_ref, value_ref, out_ref):
    out_ref[...] = value_ref[...]


def pass_after(info, value, after):
    (out,) = local_call(pass_kernel, info, (jax.ShapeDtypeStruct(value.shape, value.dtype),), SMALL_LIMIT, cost(1, 1), (value,), after=after)
    return out


def sum_kernel(info_ref, *refs):
    total = refs[0][...].astype(jnp.float32)
    for ref in refs[1:-1]:
        total += ref[...].astype(jnp.float32)
    refs[-1][...] = total.astype(jnp.bfloat16)


def rounded_sum(info, terms, after):
    out = jax.ShapeDtypeStruct(terms[0].shape, jnp.bfloat16)
    return local_call(sum_kernel, info, (out,), SMALL_LIMIT, cost(1, 1), terms, after=after)[0]


def split_kernel(info_ref, mine_ref, heard_ref, own_ref, *send_refs):
    rows = own_ref.shape[0]
    for step in range(4):
        at = pl.ds(pl.multiple_of((info_ref[5] ^ step) * rows, rows), rows)
        piece = mine_ref[at, :] + heard_ref[at, :].astype(jnp.float32)
        if step == 0:
            own_ref[...] = piece
        else:
            send_refs[step - 1][...] = piece.astype(jnp.bfloat16)


def join_kernel(info_ref, *refs):
    first_ref, second_ref = refs[8:]
    rows = refs[0].shape[0]

    def write(mine_ref, other_ref):
        for step in range(4):
            at = pl.ds(pl.multiple_of((info_ref[5] ^ step) * rows, rows), rows)
            mine_ref[at, :] = refs[step][...].astype(jnp.float32)
            other_ref[at, :] = refs[4 + step][...].astype(jnp.float32)

    @pl.when(info_ref[4] == 0)
    def _():
        write(first_ref, second_ref)

    @pl.when(info_ref[4] != 0)
    def _():
        write(second_ref, first_ref)


def coef_lanes(coef):
    slots, basis_count, steps, spans = coef.shape
    wide = jnp.pad(coef, ((0, 0), (0, 0), (0, 0), (HALO, WINDOW - HALO - spans)))
    wide = wide.reshape(slots, basis_count, steps * WINDOW)
    return jnp.pad(wide, ((0, 0), (0, 8 - basis_count), (0, LANES - steps * WINDOW)))


def edge_columns(x):
    lon_count = x.shape[-2]
    return jnp.concatenate([x[..., :EDGE, :], x[..., lon_count - EDGE :, :]], axis=-2)


def ev_swap(row):
    return lax.ppermute(row, "lat", [(i, i ^ 1) for i in range(lax.axis_size("lat"))])


def od_swap(row):
    return lax.ppermute(row, "lat", [(i, i + 1 if i % 2 else i - 1) for i in range(1, lax.axis_size("lat") - 1)])


def row_swap(ev, od):
    return ev_swap(ev), od_swap(od)


def partner(value):
    return lax.ppermute(value, "lon", [(0, 1), (1, 0)])


def across(value, step):
    size = lax.axis_size("lat")
    low = size // 4
    return lax.ppermute(value, "lat", [(i, ((i // low) ^ step) * low + i % low) for i in range(size)])


def cut_terms(info, mine, other):
    piece = jax.ShapeDtypeStruct((mine.shape[0] // 4, mine.shape[1]), jnp.bfloat16)
    outs = (jax.ShapeDtypeStruct(piece.shape, jnp.float32), piece, piece, piece)
    own, *sends = local_call(split_kernel, info, outs, SMALL_LIMIT, cost(1, 1), (mine, partner(other)))
    return own, sends


def total(info, own, sends, before_swap, before_gather, before_join):
    size = lax.axis_size("lat")
    held = rounded_sum(info, [own] + [across(sends[step - 1], step) for step in (1, 2, 3)], before_swap)
    stride = 1
    while stride < size // 4:
        heard = lax.ppermute(held, "lat", [(i, i ^ stride) for i in range(size)])
        stride *= 2
        held = rounded_sum(info, [held, heard], before_gather if stride == size // 4 else ())
    pieces = [held] + [across(held, step) for step in (1, 2, 3)]
    pieces, _ = lax.optimization_barrier((pieces, before_join))
    pieces += [partner(value) for value in pieces]
    whole = jax.ShapeDtypeStruct((4 * held.shape[0], held.shape[1]), jnp.float32)
    return local_call(join_kernel, info, (whole, whole), SMALL_LIMIT, cost(1, 1), pieces)


def per_device(state_field, heights, halo_widths, filter_values, weights_one, weights_two, cotangent):
    height = heights[0]
    spans = filter_values.shape[-1]
    channels = state_field.shape[2]
    place = lax.axis_index("lat")
    odd = lax.rem(place, 2)
    last = height - 1
    ev_row, od_row = jnp.where(odd == 1, 0, last), jnp.where(odd == 1, last, 0)

    ev = lax.dynamic_index_in_dim(state_field, ev_row, 0, keepdims=False)
    od = lax.dynamic_index_in_dim(state_field, od_row, 0, keepdims=False)
    state_ev, state_od = row_swap(ev, od)
    state_field, cotangent, halo_widths, ev, od = lax.optimization_barrier((state_field, cotangent, halo_widths, ev, od))

    info = jnp.stack([height, odd, ev_row, od_row, lax.axis_index("lon"), place // (lax.axis_size("lat") // 4)])
    info = info.astype(jnp.int32)
    offsets = jnp.abs(jnp.arange(spans, dtype=jnp.int32) - (spans - 1) // 2)
    inside = offsets[None, :] <= halo_widths[:, None]
    coef = jnp.where(inside[:, None, None, :], filter_values, jnp.zeros_like(filter_values))
    forward = coef_lanes(coef).astype(jnp.float32)
    backward = coef_lanes(coef[:, :, ::-1, ::-1])
    backward_tile = jnp.pad(backward, ((0, 0), (0, EDGE - 8), (0, 0)))
    mix_one = weights_one.reshape(3 * channels, channels)
    mix_two = weights_two.reshape(3 * channels, channels)
    mix_one_t = jnp.swapaxes(weights_one, 1, 2).reshape(3 * channels, channels)
    mix_two_t = jnp.swapaxes(weights_two, 1, 2).reshape(3 * channels, channels)

    edges_s = partner(edge_columns(state_field))
    edges_c = partner(edge_columns(cotangent))
    cot_ev = ev_swap(pack(2, info, cotangent, edges_c, backward_tile))
    cot_od = od_swap(pack(3, info, cotangent, edges_c, backward_tile, (state_ev, state_od)))
    halo_edges = partner(jnp.concatenate([edge_columns(state_ev), edge_columns(state_od)], axis=0))

    points = state_field.shape[0] * state_field.shape[1]
    flops = 2 * points * channels * (9 * WINDOW + 3 * channels)
    full, most = cost(flops, points * channels * 16), cost(3 * flops, points * channels * 24)
    basis_one, hidden, slope, ev, od = stage(
        "first", full, info, state_field, state_ev, state_od, mix_one, edges_s, halo_edges, forward
    )
    hidden_ev, hidden_od = row_swap(ev, od)
    scale = 1.0 / math.sqrt(ROWS * lax.axis_size("lat") * NLON)
    grad_pre, backward_ext, ev, od, mine, other = stage(
        "back", most, info, cotangent, cot_ev, cot_od, mix_two_t, edges_c, backward.astype(jnp.float32),
        slope, basis_one, hidden, scale=scale,
    )
    other = pass_after(info, other, (hidden_ev, hidden_od))
    own, sends = cut_terms(info, mine, other)
    grad_ev, grad_od = row_swap(ev, od)
    (next_field,) = stage("last", full, info, hidden, hidden_ev, hidden_od, mix_two, forward)
    (grad_field,) = stage("last", full, info, grad_pre, grad_ev, grad_od, mix_one_t, backward_ext)
    grad_one, grad_two = total(info, own, sends, (next_field,), (grad_ev, grad_od), grad_field)
    return next_field, grad_field, grad_one.reshape(weights_one.shape), grad_two.reshape(weights_two.shape)


def solution(mesh):
    in_specs = (
        P(("groups", "lat"), "lon", None),
        P(("groups", "lat")),
        P(("groups", "lat")),
        P(("groups", "lat"), None, None, None),
        P(),
        P(),
        P(("groups", "lat"), "lon", None),
    )
    out_specs = (
        P(("groups", "lat"), "lon", None),
        P(("groups", "lat"), "lon", None),
        P("groups", None, None),
        P("groups", None, None),
    )
    return jax.shard_map(
        per_device, mesh=mesh, in_specs=in_specs, out_specs=out_specs, check_vma=False
    )
```

```python
import functools
import math

import jax
import jax.numpy as jnp
from jax import lax
from jax.experimental import pallas as pl
from jax.experimental.pallas import tpu as pltpu
from jax.sharding import PartitionSpec as P

NLON = 1440
HALO = 8
ROWS = 2
EDGE = 2 * HALO
TILE = 48
WINDOW = TILE + 2 * EDGE
LANES = 256
CHUNKS = 3
VMEM_LIMIT = 14 * 1024 * 1024
SMALL_LIMIT = 6 * 1024 * 1024


def cost(flops, bytes_accessed):
    return pl.CostEstimate(flops=flops, bytes_accessed=bytes_accessed, transcendentals=0)


def stage_kernel(mode, transposed, scale, *refs):
    info_ref, x_ref, mix_ref = refs[:3]
    slots, channels = x_ref.shape[0], x_ref.shape[2]
    wide = x_ref.shape[1] + (0 if mode == "last" else 2 * EDGE)
    lon_count = wide - 2 * EDGE
    back = mode in ("inner", "outer")
    height, odd = info_ref[0], info_ref[1]
    own = slice(EDGE, EDGE + lon_count)
    if mode == "first":
        ev_ref, od_ref, edge_ref, halo_ref, coef_ref, basis_ref, out_ref, slope_ref, ev_out, od_out = refs[3:13]
        band_ref, xe_ref = refs[13:]
    elif mode == "inner":
        edge_ref, coef_ref, slope_ref, basis_ref, hidden_ref = refs[3:8]
        out_ref, acc_one, acc_two, band_ref, terms_ref, xe_ref, ext_ref = refs[8:]
    elif mode == "outer":
        ev_ref, od_ref, edge_ref, coef_ref, slope_ref, basis_ref, hidden_ref, _, one_ref, two_ref = refs[3:13]
        out_ref, ext_ref, ev_out, od_out, mine_ref, other_ref = refs[13:19]
        band_ref, terms_ref, xe_ref, acc_one, acc_two = refs[19:]
    else:
        ev_ref, od_ref, coef_ref, out_ref, token_ref, band_ref, terms_ref, xe_ref = refs[3:]

    def each_live(act):
        def step(row, carry):
            act(row)
            return carry

        lax.fori_loop(0, height, step, 0)

    def load(row):
        if mode == "last":
            xe_ref[row + 1] = x_ref[row]
        else:
            xe_ref[row + 1, 0:EDGE, :] = edge_ref[row, EDGE : 2 * EDGE, :]
            xe_ref[row + 1, own, :] = x_ref[row]
            xe_ref[row + 1, EDGE + lon_count : wide, :] = edge_ref[row, 0:EDGE, :]

    def load_halo(src_ref, at, slot):
        if mode == "first":
            xe_ref[slot, 0:EDGE, :] = halo_ref[at + EDGE : at + 2 * EDGE, :]
            xe_ref[slot, own, :] = src_ref[...]
            xe_ref[slot, EDGE + lon_count : wide, :] = halo_ref[at : at + EDGE, :]
        else:
            xe_ref[slot] = src_ref[0:wide, :]
        if mode == "outer":
            ext_ref[slot] = src_ref[wide : wide + EDGE, :].astype(jnp.float32)[0:8]

    each_live(load)
    if back:
        ext_ref[1 : slots + 1] = coef_ref[...]
    if mode == "inner":
        acc_one[...] = jnp.zeros_like(acc_one)
        acc_two[...] = jnp.zeros_like(acc_two)
    if mode == "outer":
        acc_one[...] = one_ref[...]
        acc_two[...] = two_ref[...]

    if mode != "inner":

        @pl.when(odd == 1)
        def _():
            load_halo(ev_ref, 0, 0)
            load_halo(od_ref, 2 * EDGE, height + 1)

        @pl.when(odd == 0)
        def _():
            load_halo(od_ref, 2 * EDGE, 0)
            load_halo(ev_ref, 0, height + 1)

    def mix(terms):
        if not transposed:
            return jnp.dot(terms, mix_ref[...], preferred_element_type=jnp.float32)
        total = None
        for k in range(3):
            span = slice(k * channels, (k + 1) * channels)
            part = lax.dot_general(
                terms[:, span], mix_ref[span, :], (((1,), (1,)), ((), ())), preferred_element_type=jnp.float32
            )
            total = part if total is None else total + part
        return total

    zeros_tail = jnp.zeros((LANES - 3 * WINDOW, channels), jnp.bfloat16)
    tiles = lon_count // TILE
    chunk = -(-tiles // CHUNKS)

    def one_row(row):
        rows_ref = ext_ref if back else coef_ref
        if rows_ref.shape[0] == slots:
            base = rows_ref[row]
        else:
            lane = lax.broadcasted_iota(jnp.int32, (8, LANES), 1)
            base = jnp.where(
                lane < WINDOW,
                rows_ref[row],
                jnp.where(lane < 2 * WINDOW, rows_ref[row + 1], rows_ref[row + 2]),
            )
        for k in range(3):
            spread = jnp.broadcast_to(base[k : k + 1], (WINDOW, LANES))
            rolled = pltpu.roll(spread, LANES - EDGE, 1, stride=1, stride_axis=0)
            band_ref[row, k * WINDOW : (k + 1) * WINDOW, :] = rolled.astype(jnp.bfloat16)

        def emit(first_tile, last_tile):
            begin, end = EDGE + first_tile * TILE, EDGE + last_tile * TILE
            if mode != "last":
                begin -= EDGE * (first_tile == 0)
                end += EDGE * (last_tile == tiles)
            for tile in range(first_tile, last_tile):
                window = jnp.concatenate(
                    [xe_ref[row + lat_step, tile * TILE : tile * TILE + WINDOW, :] for lat_step in range(3)]
                    + [zeros_tail],
                    axis=0,
                )
                low, high = EDGE, EDGE + TILE
                if mode != "last":
                    low -= EDGE * (tile == 0)
                    high += EDGE * (tile == tiles - 1)
                size = high - low
                band = jnp.concatenate(
                    [band_ref[row, k * WINDOW + low : k * WINDOW + high, :] for k in range(3)], axis=0
                )
                summed = jnp.dot(band, window, preferred_element_type=jnp.float32).astype(jnp.bfloat16)
                for k in range(3):
                    piece = summed[k * size : (k + 1) * size]
                    at = tile * TILE + low
                    span = slice(k * channels, (k + 1) * channels)
                    if mode == "first":
                        basis_ref[row, at : at + size, span] = piece
                    else:
                        terms_ref[at : at + size, span] = piece
            terms = basis_ref[row, begin:end, :] if mode == "first" else terms_ref[begin:end, :]
            mixed = mix(terms)
            if mode == "first":
                cdf = 0.5 * (1.0 + lax.erf(mixed * (1.0 / math.sqrt(2.0))))
                pdf = jnp.exp(-0.5 * mixed * mixed) * (1.0 / math.sqrt(2.0 * math.pi))
                out_ref[row, begin:end, :] = (mixed * cdf).astype(jnp.bfloat16)
                slope_ref[row, begin:end, :] = cdf + mixed * pdf
            elif back:
                out_ref[row, begin:end, :] = (mixed * slope_ref[row, begin:end, :]).astype(jnp.bfloat16)
            else:
                out_ref[row, begin - EDGE : end - EDGE, :] = mixed.astype(jnp.bfloat16)

        for first_tile in range(0, tiles, chunk):
            emit(first_tile, min(first_tile + chunk, tiles))
        if back:
            grad_t = out_ref[row, own, :].T
            hidden_t = hidden_ref[row, own, :].T
            for k in range(3):
                span = slice(k * channels, (k + 1) * channels)
                acc_one[:, span] += jnp.dot(grad_t, basis_ref[row, own, span], preferred_element_type=jnp.float32)
                acc_two[:, span] += jnp.dot(hidden_t, terms_ref[own, span], preferred_element_type=jnp.float32)

    if mode == "inner":

        def inner_row(row, carry):
            one_row(row)
            return carry

        lax.fori_loop(1, height - 1, inner_row, 0)
    elif mode == "outer":

        def outer_row(end, carry):
            one_row(end * (height - 1))
            return carry

        lax.fori_loop(0, jnp.minimum(height, 2), outer_row, 0)
    else:
        each_live(one_row)
    if mode == "last":

        def clear(row, carry):
            out_ref[row] = jnp.zeros(out_ref.shape[1:], out_ref.dtype)
            return carry

        lax.fori_loop(height, slots, clear, 0)
        token_ref[...] = jnp.zeros_like(token_ref)
    elif mode != "inner":
        ev_out[...] = out_ref[info_ref[2]]
        od_out[...] = out_ref[info_ref[3]]
        if mode == "outer":

            def write(one_ref, two_ref):
                for k in range(3):
                    span = slice(k * channels, (k + 1) * channels)
                    one_ref[span] = (acc_one[:, span].T * scale).astype(one_ref.dtype)
                    two_ref[span] = (acc_two[:, span] * scale).astype(two_ref.dtype)

            @pl.when(info_ref[4] == 0)
            def _():
                write(mine_ref, other_ref)

            @pl.when(info_ref[4] != 0)
            def _():
                write(other_ref, mine_ref)


def stage(mode, estimate, info, x, mix, *extra, transposed=False, scale=None):
    slots, channels = x.shape[0], x.shape[2]
    wide = x.shape[1] + (0 if mode == "last" else 2 * EDGE)
    lon_count = wide - 2 * EDGE
    bf16, f32 = jnp.bfloat16, jnp.float32
    vmem = pl.BlockSpec(memory_space=pltpu.VMEM)
    basis = ((slots, wide, 3 * channels), bf16)
    field = ((slots, wide, channels), bf16)
    slope = ((slots, wide, channels), f32)
    band = ((slots, 3 * WINDOW, LANES), bf16)
    row = ((wide, channels), bf16)
    terms = ((wide, 3 * channels), bf16)
    ext = ((slots + 2, wide, channels), bf16)
    sums = (3 * channels, channels)
    ext_coef = ((slots + 2, 8, LANES), f32)
    acc = ((channels, 3 * channels), f32)
    if mode == "first":
        outs = (basis, field, slope, row, row)
        scratch = [band, ext]
    elif mode == "inner":
        outs = (field, acc, acc)
        scratch = [band, terms, ext, ext_coef]
    elif mode == "outer":
        outs = (field, ext_coef, row, row, (sums, f32), (sums, bf16))
        scratch = [band, terms, ext, acc, acc]
    else:
        outs = (((slots, lon_count, channels), bf16), ((8, 128), f32))
        scratch = [band, terms, ext]
    return pl.pallas_call(
        functools.partial(stage_kernel, mode, transposed, scale),
        out_shape=tuple(jax.ShapeDtypeStruct(*array) for array in outs),
        in_specs=[pl.BlockSpec(memory_space=pltpu.SMEM)] + [vmem] * (2 + len(extra)),
        out_specs=(vmem,) * len(outs),
        scratch_shapes=[pltpu.VMEM(*array) for array in scratch],
        input_output_aliases={10: 0} if mode == "outer" else {},
        compiler_params=pltpu.CompilerParams(vmem_limit_bytes=VMEM_LIMIT),
        cost_estimate=estimate,
    )(info, x, mix, *extra)


def edge_kernel(info_ref, x_ref, out_ref):
    lon_count = x_ref.shape[1]
    out_ref[:, 0:EDGE, :] = x_ref[:, 0:EDGE, :]
    out_ref[:, EDGE : 2 * EDGE, :] = x_ref[:, lon_count - EDGE :, :]


def row_edges(info, x):
    out = jax.ShapeDtypeStruct((x.shape[0], 2 * EDGE, x.shape[2]), x.dtype)
    return local_call(edge_kernel, info, (out,), SMALL_LIMIT, cost(1, 4 * x.size), (x,))[0]


def pack_kernel(which, info_ref, x_ref, edge_ref, tile_ref, out_ref, sem):
    lon_count = x_ref.shape[1]
    wide = lon_count + 2 * EDGE
    row = info_ref[which]
    copy = pltpu.make_async_copy(x_ref.at[row], out_ref.at[EDGE : EDGE + lon_count], sem)
    copy.start()
    out_ref[0:EDGE] = edge_ref[row, EDGE : 2 * EDGE]
    out_ref[EDGE + lon_count : wide] = edge_ref[row, 0:EDGE]
    out_ref[wide : wide + EDGE] = tile_ref[row]
    copy.wait()


def pack(which, info, x, edges, tiles, after=()):
    row = jax.ShapeDtypeStruct((x.shape[1] + 3 * EDGE, x.shape[2]), x.dtype)
    kernel = functools.partial(pack_kernel, which)
    (out,) = local_call(
        kernel, info, (row,), SMALL_LIMIT, cost(0, 4 * row.size), (edges, tiles), (pltpu.SemaphoreType.DMA,), (x,), after
    )
    return out


def local_call(kernel, info, outs, limit, estimate, operands, scratch=(), far=(), after=()):
    vmem, anywhere = pl.BlockSpec(memory_space=pltpu.VMEM), pl.BlockSpec(memory_space=pl.ANY)

    def body(info_ref, *refs):
        kernel(info_ref, *refs[len(after) :])

    return pl.pallas_call(
        body,
        out_shape=tuple(outs),
        in_specs=[pl.BlockSpec(memory_space=pltpu.SMEM)]
        + [anywhere] * (len(after) + len(far))
        + [vmem] * len(operands),
        out_specs=(vmem,) * len(outs),
        scratch_shapes=list(scratch),
        compiler_params=pltpu.CompilerParams(vmem_limit_bytes=limit),
        cost_estimate=estimate,
    )(info, *after, *far, *operands)


def gate_kernel(*refs):
    pass


def gate(value, after):
    anywhere = pl.BlockSpec(memory_space=pl.ANY)
    return pl.pallas_call(
        gate_kernel,
        out_shape=jax.ShapeDtypeStruct(value.shape, value.dtype),
        in_specs=[anywhere] * (1 + len(after)),
        out_specs=anywhere,
        input_output_aliases={0: 0},
        compiler_params=pltpu.CompilerParams(vmem_limit_bytes=SMALL_LIMIT),
        cost_estimate=cost(1, 1),
    )(value, *after)


def sum_kernel(info_ref, *refs):
    total = refs[0][...].astype(jnp.float32)
    for ref in refs[1:-1]:
        total += ref[...].astype(jnp.float32)
    refs[-1][...] = total.astype(jnp.bfloat16)


def rounded_sum(info, terms, after=()):
    out = jax.ShapeDtypeStruct(terms[0].shape, jnp.bfloat16)
    return local_call(sum_kernel, info, (out,), SMALL_LIMIT, cost(1, 1), terms, after=after)[0]


def split_kernel(info_ref, mine_ref, heard_ref, own_ref, *send_refs):
    rows = own_ref.shape[0]
    for step in range(4):
        at = pl.ds(pl.multiple_of((info_ref[5] ^ step) * rows, rows), rows)
        piece = mine_ref[at, :] + heard_ref[at, :].astype(jnp.float32)
        if step == 0:
            own_ref[...] = piece
        else:
            send_refs[step - 1][...] = piece.astype(jnp.bfloat16)


def join_kernel(info_ref, *refs):
    first_ref, second_ref = refs[8:]
    rows = refs[0].shape[0]

    def write(mine_ref, other_ref):
        for step in range(4):
            at = pl.ds(pl.multiple_of((info_ref[5] ^ step) * rows, rows), rows)
            mine_ref[at, :] = refs[step][...].astype(jnp.float32)
            other_ref[at, :] = refs[4 + step][...].astype(jnp.float32)

    @pl.when(info_ref[4] == 0)
    def _():
        write(first_ref, second_ref)

    @pl.when(info_ref[4] != 0)
    def _():
        write(second_ref, first_ref)


def coef_lanes(coef):
    slots, basis_count, steps, spans = coef.shape
    wide = jnp.pad(coef, ((0, 0), (0, 0), (0, 0), (HALO, WINDOW - HALO - spans)))
    wide = wide.reshape(slots, basis_count, steps * WINDOW)
    return jnp.pad(wide, ((0, 0), (0, 8 - basis_count), (0, LANES - steps * WINDOW)))


def edge_columns(x):
    lon_count = x.shape[-2]
    return jnp.concatenate([x[..., :EDGE, :], x[..., lon_count - EDGE :, :]], axis=-2)


def ev_swap(row):
    return lax.ppermute(row, "lat", [(i, i ^ 1) for i in range(lax.axis_size("lat"))])


def od_swap(row):
    return lax.ppermute(row, "lat", [(i, i + 1 if i % 2 else i - 1) for i in range(1, lax.axis_size("lat") - 1)])


def row_swap(ev, od):
    return ev_swap(ev), od_swap(od)


def partner(value):
    return lax.ppermute(value, "lon", [(0, 1), (1, 0)])


def across(value, step):
    size = lax.axis_size("lat")
    low = size // 4
    return lax.ppermute(value, "lat", [(i, ((i // low) ^ step) * low + i % low) for i in range(size)])


def cut_terms(info, mine, other):
    piece = jax.ShapeDtypeStruct((mine.shape[0] // 4, mine.shape[1]), jnp.bfloat16)
    outs = (jax.ShapeDtypeStruct(piece.shape, jnp.float32), piece, piece, piece)
    own, *sends = local_call(split_kernel, info, outs, SMALL_LIMIT, cost(1, 1), (mine, partner(other)))
    return own, sends


def lat_sum(info, own, heard, before_first, before_last):
    size = lax.axis_size("lat")
    held = rounded_sum(info, [own] + heard, before_first)
    stride = 1
    while stride < size // 4:
        term = lax.ppermute(held, "lat", [(i, i ^ stride) for i in range(size)])
        stride *= 2
        held = rounded_sum(info, [held, term], before_last if stride == size // 4 else ())
    return held


def gather(info, held, before_join):
    pieces = [held] + [across(held, step) for step in (1, 2, 3)]
    pieces, _ = lax.optimization_barrier((pieces, before_join))
    pieces += [partner(value) for value in pieces]
    whole = jax.ShapeDtypeStruct((4 * held.shape[0], held.shape[1]), jnp.float32)
    return local_call(join_kernel, info, (whole, whole), SMALL_LIMIT, cost(1, 1), pieces)


def per_device(state_field, heights, halo_widths, filter_values, weights_one, weights_two, cotangent):
    height = heights[0]
    spans = filter_values.shape[-1]
    channels = state_field.shape[2]
    place = lax.axis_index("lat")
    odd = lax.rem(place, 2)
    last = height - 1
    ev_row, od_row = jnp.where(odd == 1, 0, last), jnp.where(odd == 1, last, 0)

    ev = lax.dynamic_index_in_dim(state_field, ev_row, 0, keepdims=False)
    od = lax.dynamic_index_in_dim(state_field, od_row, 0, keepdims=False)
    state_ev, state_od = row_swap(ev, od)
    state_field, cotangent, halo_widths, ev, od = lax.optimization_barrier((state_field, cotangent, halo_widths, ev, od))

    info = jnp.stack([height, odd, ev_row, od_row, lax.axis_index("lon"), place // (lax.axis_size("lat") // 4)])
    info = info.astype(jnp.int32)
    offsets = jnp.abs(jnp.arange(spans, dtype=jnp.int32) - (spans - 1) // 2)
    inside = offsets[None, :] <= halo_widths[:, None]
    coef = jnp.where(inside[:, None, None, :], filter_values, jnp.zeros_like(filter_values))
    forward = coef_lanes(coef).astype(jnp.float32)
    backward = coef_lanes(coef[:, :, ::-1, ::-1])
    backward_tile = jnp.pad(backward, ((0, 0), (0, EDGE - 8), (0, 0)))
    mix_one = weights_one.reshape(3 * channels, channels)
    mix_two = weights_two.reshape(3 * channels, channels)

    edges_s = partner(row_edges(info, state_field))
    edges_c = partner(row_edges(info, cotangent))
    cot_ev = ev_swap(pack(2, info, cotangent, edges_c, backward_tile))
    cot_od = od_swap(gate(pack(3, info, cotangent, edges_c, backward_tile), (state_ev, state_od)))
    halo_edges = partner(jnp.concatenate([edge_columns(state_ev), edge_columns(state_od)], axis=0))

    points = state_field.shape[0] * state_field.shape[1]
    flops = 2 * points * channels * (9 * WINDOW + 3 * channels)
    full, most = cost(flops, points * channels * 16), cost(3 * flops, points * channels * 24)
    basis_one, hidden, slope, ev, od = stage(
        "first", full, info, state_field, mix_one, state_ev, state_od, edges_s, halo_edges, forward
    )
    hidden_ev, hidden_od = ev_swap(ev), od_swap(gate(od, (cot_ev, cot_od)))
    scale = 1.0 / math.sqrt(ROWS * lax.axis_size("lat") * NLON)
    backward_wide = backward.astype(jnp.float32)
    grad_inner, inner_one, inner_two = stage(
        "inner", cost(1, 1), info, cotangent, mix_two, edges_c, backward_wide, slope, basis_one, hidden, transposed=True, scale=scale
    )
    grad_pre, backward_ext, ev, od, mine, other = stage(
        "outer", most, info, cotangent, mix_two, cot_ev, cot_od, edges_c, backward_wide, slope, basis_one, hidden,
        grad_inner, inner_one, inner_two, transposed=True, scale=scale,
    )
    own, sends = cut_terms(info, mine, gate(other, (hidden_od,)))
    heard = [across(send, step) for send, step in zip(sends, (1, 2, 3), strict=True)]
    grad_ev = ev_swap(ev)
    grad_od = od_swap(gate(od, heard))
    next_field, next_token = stage("last", full, info, hidden, mix_two, hidden_ev, hidden_od, forward)
    held = lat_sum(info, own, heard, (), (next_token, grad_ev, grad_od))
    grad_field, grad_token = stage("last", full, info, grad_pre, mix_one, grad_ev, grad_od, backward_ext, transposed=True)
    grad_one, grad_two = gather(info, held, grad_field)
    return next_field, grad_field, grad_one.reshape(weights_one.shape), grad_two.reshape(weights_two.shape)


def solution(mesh):
    in_specs = (
        P(("groups", "lat"), "lon", None),
        P(("groups", "lat")),
        P(("groups", "lat")),
        P(("groups", "lat"), None, None, None),
        P(),
        P(),
        P(("groups", "lat"), "lon", None),
    )
    out_specs = (
        P(("groups", "lat"), "lon", None),
        P(("groups", "lat"), "lon", None),
        P("groups", None, None),
        P("groups", None, None),
    )
    return jax.shard_map(
        per_device, mesh=mesh, in_specs=in_specs, out_specs=out_specs, check_vma=False
    )
```

```python
import functools
import math

import jax
import jax.numpy as jnp
from jax import lax
from jax.experimental import pallas as pl
from jax.experimental.pallas import tpu as pltpu
from jax.sharding import PartitionSpec as P

NLON = 1440
HALO = 8
ROWS = 2
EDGE = 2 * HALO
TILE = 48
WINDOW = TILE + 2 * EDGE
LANES = 256
CHUNKS = 3
VMEM_LIMIT = 14 * 1024 * 1024
SMALL_LIMIT = 6 * 1024 * 1024


def cost(flops, bytes_accessed):
    return pl.CostEstimate(flops=flops, bytes_accessed=bytes_accessed, transcendentals=0)


def stage_kernel(mode, transposed, scale, *refs):
    info_ref, x_ref, mix_ref = refs[:3]
    slots, channels = x_ref.shape[0], x_ref.shape[2]
    wide = x_ref.shape[1] + (0 if mode == "last" else 2 * EDGE)
    lon_count = wide - 2 * EDGE
    back = mode in ("inner", "outer")
    height, odd = info_ref[0], info_ref[1]
    own = slice(EDGE, EDGE + lon_count)
    if mode == "first":
        ev_ref, od_ref, edge_ref, halo_ref, coef_ref, basis_ref, out_ref, slope_ref, ev_out, od_out = refs[3:13]
        band_ref, xe_ref = refs[13:]
    elif mode == "inner":
        edge_ref, coef_ref, slope_ref, basis_ref, hidden_ref = refs[3:8]
        out_ref, acc_one, acc_two, band_ref, terms_ref, xe_ref, ext_ref = refs[8:]
    elif mode == "outer":
        ev_ref, od_ref, edge_ref, coef_ref, slope_ref, basis_ref, hidden_ref, _, one_ref, two_ref = refs[3:13]
        out_ref, ext_ref, ev_out, od_out, mine_ref, other_ref = refs[13:19]
        band_ref, terms_ref, xe_ref, acc_one, acc_two = refs[19:]
    else:
        ev_ref, od_ref, coef_ref, out_ref, token_ref, band_ref, terms_ref, xe_ref = refs[3:]

    def each_live(act):
        def step(row, carry):
            act(row)
            return carry

        lax.fori_loop(0, height, step, 0)

    def load(row):
        if mode == "last":
            xe_ref[row + 1] = x_ref[row]
        else:
            xe_ref[row + 1, 0:EDGE, :] = edge_ref[row, EDGE : 2 * EDGE, :]
            xe_ref[row + 1, own, :] = x_ref[row]
            xe_ref[row + 1, EDGE + lon_count : wide, :] = edge_ref[row, 0:EDGE, :]

    def load_halo(src_ref, at, slot):
        if mode == "first":
            xe_ref[slot, 0:EDGE, :] = halo_ref[at + EDGE : at + 2 * EDGE, :]
            xe_ref[slot, own, :] = src_ref[...]
            xe_ref[slot, EDGE + lon_count : wide, :] = halo_ref[at : at + EDGE, :]
        else:
            xe_ref[slot] = src_ref[0:wide, :]
        if mode == "outer":
            ext_ref[slot] = src_ref[wide : wide + EDGE, :].astype(jnp.float32)[0:8]

    each_live(load)
    if back:
        ext_ref[1 : slots + 1] = coef_ref[...]
    if mode == "inner":
        acc_one[...] = jnp.zeros_like(acc_one)
        acc_two[...] = jnp.zeros_like(acc_two)
    if mode == "outer":
        acc_one[...] = one_ref[...]
        acc_two[...] = two_ref[...]

    if mode != "inner":

        @pl.when(odd == 1)
        def _():
            load_halo(ev_ref, 0, 0)
            load_halo(od_ref, 2 * EDGE, height + 1)

        @pl.when(odd == 0)
        def _():
            load_halo(od_ref, 2 * EDGE, 0)
            load_halo(ev_ref, 0, height + 1)

    def mix(terms):
        if not transposed:
            return jnp.dot(terms, mix_ref[...], preferred_element_type=jnp.float32)
        total = None
        for k in range(3):
            span = slice(k * channels, (k + 1) * channels)
            part = lax.dot_general(
                terms[:, span], mix_ref[span, :], (((1,), (1,)), ((), ())), preferred_element_type=jnp.float32
            )
            total = part if total is None else total + part
        return total

    zeros_tail = jnp.zeros((LANES - 3 * WINDOW, channels), jnp.bfloat16)
    tiles = lon_count // TILE
    chunk = -(-tiles // CHUNKS)

    def one_row(row):
        rows_ref = ext_ref if back else coef_ref
        if rows_ref.shape[0] == slots:
            base = rows_ref[row]
        else:
            lane = lax.broadcasted_iota(jnp.int32, (8, LANES), 1)
            base = jnp.where(
                lane < WINDOW,
                rows_ref[row],
                jnp.where(lane < 2 * WINDOW, rows_ref[row + 1], rows_ref[row + 2]),
            )
        for k in range(3):
            spread = jnp.broadcast_to(base[k : k + 1], (WINDOW, LANES))
            rolled = pltpu.roll(spread, LANES - EDGE, 1, stride=1, stride_axis=0)
            band_ref[row, k * WINDOW : (k + 1) * WINDOW, :] = rolled.astype(jnp.bfloat16)

        def emit(first_tile, last_tile):
            begin, end = EDGE + first_tile * TILE, EDGE + last_tile * TILE
            if mode != "last":
                begin -= EDGE * (first_tile == 0)
                end += EDGE * (last_tile == tiles)
            for tile in range(first_tile, last_tile):
                window = jnp.concatenate(
                    [xe_ref[row + lat_step, tile * TILE : tile * TILE + WINDOW, :] for lat_step in range(3)]
                    + [zeros_tail],
                    axis=0,
                )
                low, high = EDGE, EDGE + TILE
                if mode != "last":
                    low -= EDGE * (tile == 0)
                    high += EDGE * (tile == tiles - 1)
                size = high - low
                band = jnp.concatenate(
                    [band_ref[row, k * WINDOW + low : k * WINDOW + high, :] for k in range(3)], axis=0
                )
                summed = jnp.dot(band, window, preferred_element_type=jnp.float32).astype(jnp.bfloat16)
                for k in range(3):
                    piece = summed[k * size : (k + 1) * size]
                    at = tile * TILE + low
                    span = slice(k * channels, (k + 1) * channels)
                    if mode == "first":
                        basis_ref[row, at : at + size, span] = piece
                    else:
                        terms_ref[at : at + size, span] = piece
            terms = basis_ref[row, begin:end, :] if mode == "first" else terms_ref[begin:end, :]
            mixed = mix(terms)
            if mode == "first":
                cdf = 0.5 * (1.0 + lax.erf(mixed * (1.0 / math.sqrt(2.0))))
                pdf = jnp.exp(-0.5 * mixed * mixed) * (1.0 / math.sqrt(2.0 * math.pi))
                out_ref[row, begin:end, :] = (mixed * cdf).astype(jnp.bfloat16)
                slope_ref[row, begin:end, :] = cdf + mixed * pdf
            elif back:
                out_ref[row, begin:end, :] = (mixed * slope_ref[row, begin:end, :]).astype(jnp.bfloat16)
            else:
                out_ref[row, begin - EDGE : end - EDGE, :] = mixed.astype(jnp.bfloat16)

        for first_tile in range(0, tiles, chunk):
            emit(first_tile, min(first_tile + chunk, tiles))
        if back:
            grad_t = out_ref[row, own, :].T
            hidden_t = hidden_ref[row, own, :].T
            for k in range(3):
                span = slice(k * channels, (k + 1) * channels)
                acc_one[:, span] += jnp.dot(grad_t, basis_ref[row, own, span], preferred_element_type=jnp.float32)
                acc_two[:, span] += jnp.dot(hidden_t, terms_ref[own, span], preferred_element_type=jnp.float32)

    if mode == "inner":

        def inner_row(row, carry):
            one_row(row)
            return carry

        lax.fori_loop(1, height - 1, inner_row, 0)
    elif mode == "outer":

        def outer_row(end, carry):
            one_row(end * (height - 1))
            return carry

        lax.fori_loop(0, jnp.minimum(height, 2), outer_row, 0)
    else:
        each_live(one_row)
    if mode == "last":

        def clear(row, carry):
            out_ref[row] = jnp.zeros(out_ref.shape[1:], out_ref.dtype)
            return carry

        lax.fori_loop(height, slots, clear, 0)
        token_ref[...] = jnp.zeros_like(token_ref)
    elif mode != "inner":
        ev_out[...] = out_ref[info_ref[2]]
        od_out[...] = out_ref[info_ref[3]]
        if mode == "outer":

            def write(one_ref, two_ref):
                for k in range(3):
                    span = slice(k * channels, (k + 1) * channels)
                    one_ref[span] = (acc_one[:, span].T * scale).astype(one_ref.dtype)
                    two_ref[span] = (acc_two[:, span] * scale).astype(two_ref.dtype)

            @pl.when(info_ref[4] == 0)
            def _():
                write(mine_ref, other_ref)

            @pl.when(info_ref[4] != 0)
            def _():
                write(other_ref, mine_ref)


def stage(mode, estimate, info, x, mix, *extra, transposed=False, scale=None):
    slots, channels = x.shape[0], x.shape[2]
    wide = x.shape[1] + (0 if mode == "last" else 2 * EDGE)
    lon_count = wide - 2 * EDGE
    bf16, f32 = jnp.bfloat16, jnp.float32
    vmem = pl.BlockSpec(memory_space=pltpu.VMEM)
    basis = ((slots, wide, 3 * channels), bf16)
    field = ((slots, wide, channels), bf16)
    slope = ((slots, wide, channels), f32)
    band = ((slots, 3 * WINDOW, LANES), bf16)
    row = ((wide, channels), bf16)
    terms = ((wide, 3 * channels), bf16)
    ext = ((slots + 2, wide, channels), bf16)
    sums = (3 * channels, channels)
    ext_coef = ((slots + 2, 8, LANES), f32)
    acc = ((channels, 3 * channels), f32)
    if mode == "first":
        outs = (basis, field, slope, row, row)
        scratch = [band, ext]
    elif mode == "inner":
        outs = (field, acc, acc)
        scratch = [band, terms, ext, ext_coef]
    elif mode == "outer":
        outs = (field, ext_coef, row, row, (sums, f32), (sums, bf16))
        scratch = [band, terms, ext, acc, acc]
    else:
        outs = (((slots, lon_count, channels), bf16), ((8, 128), f32))
        scratch = [band, terms, ext]
    return pl.pallas_call(
        functools.partial(stage_kernel, mode, transposed, scale),
        out_shape=tuple(jax.ShapeDtypeStruct(*array) for array in outs),
        in_specs=[pl.BlockSpec(memory_space=pltpu.SMEM)] + [vmem] * (2 + len(extra)),
        out_specs=(vmem,) * len(outs),
        scratch_shapes=[pltpu.VMEM(*array) for array in scratch],
        input_output_aliases={10: 0} if mode == "outer" else {},
        compiler_params=pltpu.CompilerParams(vmem_limit_bytes=VMEM_LIMIT),
        cost_estimate=estimate,
    )(info, x, mix, *extra)


def edge_kernel(info_ref, x_ref, out_ref):
    lon_count = x_ref.shape[1]
    out_ref[:, 0:EDGE, :] = x_ref[:, 0:EDGE, :]
    out_ref[:, EDGE : 2 * EDGE, :] = x_ref[:, lon_count - EDGE :, :]


def row_edges(info, x):
    out = jax.ShapeDtypeStruct((x.shape[0], 2 * EDGE, x.shape[2]), x.dtype)
    return local_call(edge_kernel, info, (out,), SMALL_LIMIT, cost(1, 4 * x.size), (x,))[0]


def pack_kernel(which, info_ref, x_ref, edge_ref, tile_ref, out_ref, sem):
    lon_count = x_ref.shape[1]
    wide = lon_count + 2 * EDGE
    row = info_ref[which]
    copy = pltpu.make_async_copy(x_ref.at[row], out_ref.at[EDGE : EDGE + lon_count], sem)
    copy.start()
    out_ref[0:EDGE] = edge_ref[row, EDGE : 2 * EDGE]
    out_ref[EDGE + lon_count : wide] = edge_ref[row, 0:EDGE]
    out_ref[wide : wide + EDGE] = tile_ref[row]
    copy.wait()


def pack(which, info, x, edges, tiles, after=()):
    row = jax.ShapeDtypeStruct((x.shape[1] + 3 * EDGE, x.shape[2]), x.dtype)
    kernel = functools.partial(pack_kernel, which)
    (out,) = local_call(
        kernel, info, (row,), SMALL_LIMIT, cost(0, 4 * row.size), (edges, tiles), (pltpu.SemaphoreType.DMA,), (x,), after
    )
    return out


def local_call(kernel, info, outs, limit, estimate, operands, scratch=(), far=(), after=()):
    vmem, anywhere = pl.BlockSpec(memory_space=pltpu.VMEM), pl.BlockSpec(memory_space=pl.ANY)

    def body(info_ref, *refs):
        kernel(info_ref, *refs[len(after) :])

    return pl.pallas_call(
        body,
        out_shape=tuple(outs),
        in_specs=[pl.BlockSpec(memory_space=pltpu.SMEM)]
        + [anywhere] * (len(after) + len(far))
        + [vmem] * len(operands),
        out_specs=(vmem,) * len(outs),
        scratch_shapes=list(scratch),
        compiler_params=pltpu.CompilerParams(vmem_limit_bytes=limit),
        cost_estimate=estimate,
    )(info, *after, *far, *operands)


def gate_kernel(*refs):
    pass


def gate(value, after):
    anywhere = pl.BlockSpec(memory_space=pl.ANY)
    return pl.pallas_call(
        gate_kernel,
        out_shape=jax.ShapeDtypeStruct(value.shape, value.dtype),
        in_specs=[anywhere] * (1 + len(after)),
        out_specs=anywhere,
        input_output_aliases={0: 0},
        compiler_params=pltpu.CompilerParams(vmem_limit_bytes=SMALL_LIMIT),
        cost_estimate=cost(1, 1),
    )(value, *after)


def sum_kernel(info_ref, *refs):
    total = refs[0][...].astype(jnp.float32)
    for ref in refs[1:-1]:
        total += ref[...].astype(jnp.float32)
    refs[-1][...] = total.astype(jnp.bfloat16)


def rounded_sum(info, terms, after=()):
    out = jax.ShapeDtypeStruct(terms[0].shape, jnp.bfloat16)
    return local_call(sum_kernel, info, (out,), SMALL_LIMIT, cost(1, 1), terms, after=after)[0]


def split_kernel(info_ref, mine_ref, heard_ref, own_ref, *send_refs):
    rows = own_ref.shape[0]
    for step in range(4):
        at = pl.ds(pl.multiple_of((info_ref[5] ^ step) * rows, rows), rows)
        piece = mine_ref[at, :] + heard_ref[at, :].astype(jnp.float32)
        if step == 0:
            own_ref[...] = piece
        else:
            send_refs[step - 1][...] = piece.astype(jnp.bfloat16)


def join_kernel(info_ref, *refs):
    first_ref, second_ref = refs[8:]
    rows = refs[0].shape[0]

    def write(mine_ref, other_ref):
        for step in range(4):
            at = pl.ds(pl.multiple_of((info_ref[5] ^ step) * rows, rows), rows)
            mine_ref[at, :] = refs[step][...].astype(jnp.float32)
            other_ref[at, :] = refs[4 + step][...].astype(jnp.float32)

    @pl.when(info_ref[4] == 0)
    def _():
        write(first_ref, second_ref)

    @pl.when(info_ref[4] != 0)
    def _():
        write(second_ref, first_ref)


def coef_lanes(coef):
    slots, basis_count, steps, spans = coef.shape
    wide = jnp.pad(coef, ((0, 0), (0, 0), (0, 0), (HALO, WINDOW - HALO - spans)))
    wide = wide.reshape(slots, basis_count, steps * WINDOW)
    return jnp.pad(wide, ((0, 0), (0, 8 - basis_count), (0, LANES - steps * WINDOW)))


def edge_columns(x):
    lon_count = x.shape[-2]
    return jnp.concatenate([x[..., :EDGE, :], x[..., lon_count - EDGE :, :]], axis=-2)


def ev_swap(row):
    return lax.ppermute(row, "lat", [(i, i ^ 1) for i in range(lax.axis_size("lat"))])


def od_swap(row):
    return lax.ppermute(row, "lat", [(i, i + 1 if i % 2 else i - 1) for i in range(1, lax.axis_size("lat") - 1)])


def row_swap(ev, od):
    return ev_swap(ev), od_swap(od)


def partner(value):
    return lax.ppermute(value, "lon", [(0, 1), (1, 0)])


def across(value, step):
    size = lax.axis_size("lat")
    low = size // 4
    return lax.ppermute(value, "lat", [(i, ((i // low) ^ step) * low + i % low) for i in range(size)])


def cut_terms(info, mine, other):
    piece = jax.ShapeDtypeStruct((mine.shape[0] // 4, mine.shape[1]), jnp.bfloat16)
    outs = (jax.ShapeDtypeStruct(piece.shape, jnp.float32), piece, piece, piece)
    own, *sends = local_call(split_kernel, info, outs, SMALL_LIMIT, cost(1, 1), (mine, partner(other)))
    return own, sends


def lat_sum(info, own, heard, before_first, before_last):
    size = lax.axis_size("lat")
    held, term = rounded_sum(info, [own] + heard, before_first), heard[-1]
    stride = 1
    while stride < size // 4:
        term = lax.ppermute(held, "lat", [(i, i ^ stride) for i in range(size)])
        stride *= 2
        held = rounded_sum(info, [held, term], before_last if stride == size // 4 else ())
    return held, term


def gather(info, held, before_join):
    pieces = [held] + [across(held, step) for step in (1, 2, 3)]
    pieces, _ = lax.optimization_barrier((pieces, before_join))
    pieces += [partner(value) for value in pieces]
    whole = jax.ShapeDtypeStruct((4 * held.shape[0], held.shape[1]), jnp.float32)
    return local_call(join_kernel, info, (whole, whole), SMALL_LIMIT, cost(1, 1), pieces)


def per_device(state_field, heights, halo_widths, filter_values, weights_one, weights_two, cotangent):
    height = heights[0]
    spans = filter_values.shape[-1]
    channels = state_field.shape[2]
    place = lax.axis_index("lat")
    odd = lax.rem(place, 2)
    last = height - 1
    ev_row, od_row = jnp.where(odd == 1, 0, last), jnp.where(odd == 1, last, 0)

    ev = lax.dynamic_index_in_dim(state_field, ev_row, 0, keepdims=False)
    od = lax.dynamic_index_in_dim(state_field, od_row, 0, keepdims=False)
    state_ev, state_od = row_swap(ev, od)
    state_field, cotangent, halo_widths, ev, od = lax.optimization_barrier((state_field, cotangent, halo_widths, ev, od))

    info = jnp.stack([height, odd, ev_row, od_row, lax.axis_index("lon"), place // (lax.axis_size("lat") // 4)])
    info = info.astype(jnp.int32)
    offsets = jnp.abs(jnp.arange(spans, dtype=jnp.int32) - (spans - 1) // 2)
    inside = offsets[None, :] <= halo_widths[:, None]
    coef = jnp.where(inside[:, None, None, :], filter_values, jnp.zeros_like(filter_values))
    forward = coef_lanes(coef).astype(jnp.float32)
    backward = coef_lanes(coef[:, :, ::-1, ::-1])
    backward_tile = jnp.pad(backward, ((0, 0), (0, EDGE - 8), (0, 0)))
    mix_one = weights_one.reshape(3 * channels, channels)
    mix_two = weights_two.reshape(3 * channels, channels)

    edges_s = partner(row_edges(info, state_field))
    edges_c = partner(row_edges(info, cotangent))
    cot_ev = ev_swap(pack(2, info, cotangent, edges_c, backward_tile))
    cot_od = od_swap(gate(pack(3, info, cotangent, edges_c, backward_tile), (state_ev, state_od)))
    halo_edges = partner(jnp.concatenate([edge_columns(state_ev), edge_columns(state_od)], axis=0))

    points = state_field.shape[0] * state_field.shape[1]
    flops = 2 * points * channels * (9 * WINDOW + 3 * channels)
    full, most = cost(flops, points * channels * 16), cost(3 * flops, points * channels * 24)
    basis_one, hidden, slope, ev, od = stage(
        "first", full, info, state_field, mix_one, state_ev, state_od, edges_s, halo_edges, forward
    )
    hidden_ev, hidden_od = ev_swap(ev), od_swap(gate(od, (cot_ev, cot_od)))
    scale = 1.0 / math.sqrt(ROWS * lax.axis_size("lat") * NLON)
    backward_wide = backward.astype(jnp.float32)
    grad_inner, inner_one, inner_two = stage(
        "inner", cost(1, 1), info, cotangent, mix_two, edges_c, backward_wide, slope, basis_one, hidden, transposed=True, scale=scale
    )
    grad_pre, backward_ext, ev, od, mine, other = stage(
        "outer", most, info, cotangent, mix_two, cot_ev, cot_od, edges_c, backward_wide, slope, basis_one, hidden,
        grad_inner, inner_one, inner_two, transposed=True, scale=scale,
    )
    own, sends = cut_terms(info, mine, gate(other, (hidden_od,)))
    heard = [across(send, step) for send, step in zip(sends, (1, 2, 3), strict=True)]
    grad_od = od_swap(gate(od, heard))
    next_field, next_token = stage("last", full, info, hidden, mix_two, hidden_ev, hidden_od, forward)
    held, term = lat_sum(info, own, heard, (), ())
    grad_ev = ev_swap(gate(ev, (term,)))
    grad_field, grad_token = stage("last", full, info, grad_pre, mix_one, grad_ev, grad_od, backward_ext, transposed=True)
    grad_one, grad_two = gather(info, held, (next_field, grad_field))
    return next_field, grad_field, grad_one.reshape(weights_one.shape), grad_two.reshape(weights_two.shape)


def solution(mesh):
    in_specs = (
        P(("groups", "lat"), "lon", None),
        P(("groups", "lat")),
        P(("groups", "lat")),
        P(("groups", "lat"), None, None, None),
        P(),
        P(),
        P(("groups", "lat"), "lon", None),
    )
    out_specs = (
        P(("groups", "lat"), "lon", None),
        P(("groups", "lat"), "lon", None),
        P("groups", None, None),
        P("groups", None, None),
    )
    return jax.shard_map(
        per_device, mesh=mesh, in_specs=in_specs, out_specs=out_specs, check_vma=False
    )
```
